32 devices in a mesh: row: 4 (over y, core), col: 8 (over z, x).
Axes of the slice: x: 2, y: 2, z: 4, core: 2. Of those that a mesh axis runs over, the one named last changes fastest.
Arguments:
- tokens: bfloat16 [1024, 6144], P('row', 'col'), may hold values from -6 to 6
- cotangent: bfloat16 [1024, 6144], P('row', 'col'), may hold values from -6 to 6
- w_expand: bfloat16 [6144, 12288], P('row', 'col'), may hold values from -0.078125 to 0.078125
- w_reduce: bfloat16 [6144, 12288], P('row', 'col'), may hold values from -0.0546875 to 0.0546875
- expand_mean: bfloat16 [6144, 12288], P('row', 'col'), may hold values from -1 to 1
- expand_mean_scale: float32 [24, 12288], P('row', 'col'), may hold values from 4 to 16
- expand_var: bfloat16 [6144, 12288], P('row', 'col'), may hold values from 0.049804688 to 1
- expand_var_scale: float32 [24, 12288], P('row', 'col'), may hold values from 4 to 16
- reduce_mean: bfloat16 [6144, 12288], P('row', 'col'), may hold values from -1 to 1
- reduce_mean_scale: float32 [24, 12288], P('row', 'col'), may hold values from 4 to 16
- reduce_var: bfloat16 [6144, 12288], P('row', 'col'), may hold values from 0.049804688 to 1
- reduce_var_scale: float32 [24, 12288], P('row', 'col'), may hold values from 4 to 16
Outputs:
- grad_tokens: bfloat16 [1024, 6144], P('row', 'col')
- new_expand: bfloat16 [6144, 12288], P('row', 'col')
- expand_mean_next: bfloat16 [6144, 12288], P('row', 'col')
- expand_mean_scale_next: float32 [24, 12288], P('row', 'col')
- expand_var_next: bfloat16 [6144, 12288], P('row', 'col')
- expand_var_scale_next: float32 [24, 12288], P('row', 'col')
- new_reduce: bfloat16 [6144, 12288], P('row', 'col')
- reduce_mean_next: bfloat16 [6144, 12288], P('row', 'col')
- reduce_mean_scale_next: float32 [24, 12288], P('row', 'col')
- reduce_var_next: bfloat16 [6144, 12288], P('row', 'col')
- reduce_var_scale_next: float32 [24, 12288], P('row', 'col')
The draws below stay inside these ranges and needn't reach their ends.
All inputs are finite; a program needn't handle non-finite values.
Results may differ from the reference program's by a relative error of at most 0.0049.
Values may be sent and summed in bfloat16 or wider, within the bound.
A program may use at most 192 MiB of HBM per device.

```python
import math
import jax
import jax.numpy as jnp
from jax import lax

D = 6144
FF = 12288
STEP = 10
TOKENS = 1024
NBLK = 24


def block_levels(key, dims, pieces, low, top_value):
    level = 1.0
    for position, parts in pieces:
        draws = jax.random.uniform(jax.random.fold_in(jax.random.fold_in(key, 6), position), (parts,), jnp.float32, low / len(pieces), top_value / len(pieces))
        level = level * jnp.repeat(jnp.exp(draws), dims[position] // parts).reshape((-1,) + (1,) * (len(dims) - 1 - position))
    return level


def gaussian(rng, shape, scale, bound, split=(), dtype=jnp.bfloat16):
    values = scale * jax.random.normal(rng, shape, jnp.float32)
    if split:
        values = values * block_levels(rng, shape, split, -0.22, 0.18)
    return jnp.clip(values, -bound, bound).astype(dtype)


def setup_inputs(seed: int = 0) -> dict:
    seeds = jax.random.split(jax.random.key(seed), 13)
    tokens = gaussian(seeds[0], (TOKENS, D), 1.0, 6.0, ((0, 4), (1, 8)))
    cotangent = gaussian(seeds[1], (TOKENS, D), 1.0, 6.0, ((0, 4), (1, 8)))
    w_expand = gaussian(seeds[2], (D, FF), D ** -0.5, 0.078125, ((0, 4), (1, 8)))
    w_reduce = gaussian(seeds[3], (D, FF), FF ** -0.5, 0.0546875, ((0, 4), (1, 8)))
    expand_mean = jnp.clip(jax.random.uniform(seeds[4], (D, FF), jnp.float32, -1.0, 1.0) * block_levels(seeds[4], (D, FF), ((0, 4), (1, 8)), -0.4, 0.0), -1.0, 1.0).astype(jnp.bfloat16)
    expand_mean_scale = jnp.clip(jnp.exp(math.log(16.0) - 1.3862944 * jax.random.uniform(seeds[5], (NBLK, FF), jnp.float32) ** block_levels(seeds[5], (NBLK, FF), ((0, 4), (1, 8)), -0.2, 0.2)), 4.0, 16.0)
    expand_var = jnp.clip(0.049804688 + 0.9501953 * jax.random.uniform(seeds[6], (D, FF), jnp.float32) ** block_levels(seeds[6], (D, FF), ((0, 4), (1, 8)), -0.2, 0.2), 0.049804688, 1.0).astype(jnp.bfloat16)
    expand_var_scale = jnp.clip(jnp.exp(math.log(16.0) - 1.3862944 * jax.random.uniform(seeds[7], (NBLK, FF), jnp.float32) ** block_levels(seeds[7], (NBLK, FF), ((0, 4), (1, 8)), -0.2, 0.2)), 4.0, 16.0)
    reduce_mean = jnp.clip(jax.random.uniform(seeds[8], (D, FF), jnp.float32, -1.0, 1.0) * block_levels(seeds[8], (D, FF), ((0, 4), (1, 8)), -0.4, 0.0), -1.0, 1.0).astype(jnp.bfloat16)
    reduce_mean_scale = jnp.clip(jnp.exp(math.log(16.0) - 1.3862944 * jax.random.uniform(seeds[9], (NBLK, FF), jnp.float32) ** block_levels(seeds[9], (NBLK, FF), ((0, 4), (1, 8)), -0.2, 0.2)), 4.0, 16.0)
    reduce_var = jnp.clip(0.049804688 + 0.9501953 * jax.random.uniform(seeds[10], (D, FF), jnp.float32) ** block_levels(seeds[10], (D, FF), ((0, 4), (1, 8)), -0.2, 0.2), 0.049804688, 1.0).astype(jnp.bfloat16)
    reduce_var_scale = jnp.clip(jnp.exp(math.log(16.0) - 1.3862944 * jax.random.uniform(seeds[11], (NBLK, FF), jnp.float32) ** block_levels(seeds[11], (NBLK, FF), ((0, 4), (1, 8)), -0.2, 0.2)), 4.0, 16.0)
    return {"tokens": tokens, "cotangent": cotangent, "w_expand": w_expand, "w_reduce": w_reduce, "expand_mean": expand_mean, "expand_mean_scale": expand_mean_scale, "expand_var": expand_var, "expand_var_scale": expand_var_scale, "reduce_mean": reduce_mean, "reduce_mean_scale": reduce_mean_scale, "reduce_var": reduce_var, "reduce_var_scale": reduce_var_scale}


beta_one = 0.9
beta_two = 0.999
adam_eps = 1e-08
learn_rate = 0.001
decay_rate = 0.1
scale_eps = 1e-06

def gelu_pair(pre_act):
    cdf_part = 0.5 * (1.0 + lax.erf(pre_act * 0.7071067811865476))
    slope = cdf_part + pre_act * jnp.exp(-0.5 * pre_act * pre_act) * 0.3989422804014327
    return (pre_act * cdf_part, slope)

def spread_scale(values, scale):
    blocks = scale.shape[0]
    shaped = values.reshape(blocks, values.shape[0] // blocks, values.shape[1])
    return (shaped * scale[:, None, :]).reshape(values.shape)

def block_max(values, blocks):
    shaped = values.reshape(blocks, values.shape[0] // blocks, values.shape[1])
    return lax.optimization_barrier(jnp.max(jnp.abs(shaped), axis=1)) + scale_eps

def adam_step(weight, grad_w, mean_q, mean_scale, var_q, var_scale):
    blocks = mean_scale.shape[0]
    mean_new = beta_one * spread_scale(mean_q.astype(jnp.float32), mean_scale) + (1.0 - beta_one) * grad_w
    var_new = beta_two * spread_scale(var_q.astype(jnp.float32), var_scale) + (1.0 - beta_two) * grad_w * grad_w
    mean_hat = mean_new / (1.0 - beta_one ** STEP)
    var_hat = var_new / (1.0 - beta_two ** STEP)
    old_weight = weight.astype(jnp.float32)
    new_weight = (old_weight - learn_rate * (mean_hat / (jnp.sqrt(var_hat) + adam_eps) + decay_rate * old_weight)).astype(jnp.bfloat16)
    mean_scale_next = block_max(mean_new, blocks)
    var_scale_next = block_max(var_new, blocks)
    mean_next = spread_scale(mean_new, 1.0 / mean_scale_next).astype(jnp.bfloat16)
    var_next = spread_scale(var_new, 1.0 / var_scale_next).astype(jnp.bfloat16)
    return (new_weight, mean_next, mean_scale_next, var_next, var_scale_next)

def reference(tokens, cotangent, w_expand, w_reduce, expand_mean, expand_mean_scale, expand_var, expand_var_scale, reduce_mean, reduce_mean_scale, reduce_var, reduce_var_scale):
    pre_act = jnp.dot(tokens, w_expand, preferred_element_type=jnp.float32)
    activated, slope = gelu_pair(pre_act)
    activated = activated.astype(jnp.bfloat16)
    act_grad = jnp.dot(cotangent, w_reduce, preferred_element_type=jnp.float32)
    pre_grad = (act_grad * slope).astype(jnp.bfloat16)
    grad_tokens = jnp.dot(pre_grad, w_expand.T, preferred_element_type=jnp.float32).astype(jnp.bfloat16)
    grad_expand = jnp.dot(tokens.T, pre_grad, preferred_element_type=jnp.float32)
    grad_reduce = jnp.dot(cotangent.T, activated, preferred_element_type=jnp.float32)
    first = adam_step(w_expand, grad_expand, expand_mean, expand_mean_scale, expand_var, expand_var_scale)
    second = adam_step(w_reduce, grad_reduce, reduce_mean, reduce_mean_scale, reduce_var, reduce_var_scale)
    return (grad_tokens, first[0], first[1], first[2], first[3], first[4], second[0], second[1], second[2], second[3], second[4])
```

```python
import functools

import jax
import jax.numpy as jnp
from jax import lax
from jax.experimental import pallas as pl
from jax.experimental.pallas import tpu as pltpu
from jax.sharding import PartitionSpec as P

STEP = 10


beta_one = 0.9
beta_two = 0.999
adam_eps = 1e-08
learn_rate = 0.001
decay_rate = 0.1
scale_eps = 1e-06

MESH = pl.DeviceIdType.MESH
F32 = jnp.float32
BF16 = jnp.bfloat16


def gelu_pair(pre_act):
    cdf_part = 0.5 * (1.0 + lax.erf(pre_act * 0.7071067811865476))
    slope = cdf_part + pre_act * jnp.exp(-0.5 * pre_act * pre_act) * 0.3989422804014327
    return (pre_act * cdf_part, slope)


def ring_place(col, n):
    half, odd = col // 2, col % 2
    return half * (1 - odd) + (n - 1 - half) * odd


def ring_col(place, n):
    place = lax.rem(place + 2 * n, n)
    back = place // (n // 2)
    return (1 - back) * 2 * place + back * (2 * (n - 1 - place) + 1)


def greet(peers):
    barrier = pltpu.get_barrier_semaphore()
    for peer in peers:
        pl.semaphore_signal(barrier, inc=1, device_id=peer, device_id_type=MESH)
    pl.semaphore_wait(barrier, len(peers))


def forward_kernel(
    nrow, ncol,
    tok_ref, cot_ref, we_ref, wr_ref,
    tok_all, cot_all, pg_all, ac_all,
    w_tile, total, send_one, recv_one, send_two, recv_two,
    w_sem, ring_send, ring_recv, one_send, one_recv, two_send, two_recv, out_send, out_recv,
):
    ny = nrow // 2
    half = ncol // 2
    rows = tok_ref.shape[0]
    width = w_tile.shape[3]
    me_c = lax.axis_index("col")
    me_r = lax.axis_index("row")
    y, core = me_r // 2, me_r % 2
    place = ring_place(me_c, ncol)
    right, left = ring_col(place + 1, ncol), ring_col(place - 1, ncol)
    sibling = y * 2 + 1 - core
    others = [lax.rem(y + step, ny) * 2 + core for step in range(1, ny)]

    loads = [
        pltpu.make_async_copy(ref, w_tile.at[i], w_sem.at[i])
        for i, ref in enumerate((we_ref, wr_ref))
    ]
    for load in loads:
        load.start()
    greet([{"col": left}, {"col": right}, {"row": sibling}] + [{"row": o} for o in others])

    gathered = (tok_all, cot_all)
    tok_all[me_c] = tok_ref[...]
    cot_all[me_c] = cot_ref[...]

    def hop(way, step, which, origin):
        slot = ring_col(place + origin, ncol)
        return pltpu.make_async_remote_copy(
            src_ref=gathered[which].at[slot],
            dst_ref=gathered[which].at[slot],
            send_sem=ring_send.at[way, step - 1, which],
            recv_sem=ring_recv.at[way, step - 1, which],
            device_id={"col": right if way == 0 else left},
            device_id_type=MESH,
        )

    def carried(way, step):
        return (0, 1) if step < half else (way,)

    def origin_of(way, distance):
        return -distance if way == 0 else distance

    sent = []
    for which in (0, 1):
        for way in (0, 1):
            if which in carried(way, 1):
                copy = hop(way, 1, which, 0)
                copy.start()
                sent.append(copy)

    tile = width // 3
    total[...] = jnp.zeros_like(total)
    for load in loads:
        load.wait()

    def multiply(which, origin):
        slot = ring_col(place + origin, ncol)
        part, band = slot // nrow, slot % nrow

        @pl.loop(0, 3)
        def _(j):
            cols = pl.ds(pl.multiple_of(j * tile, 128), tile)
            total[which, band, :, cols] += jnp.dot(
                gathered[which][slot], w_tile[which, part, :, cols], preferred_element_type=F32
            )

    multiply(0, 0)
    multiply(1, 0)
    for step in range(1, half + 1):
        for which in (0, 1):
            for way in (0, 1):
                if which in carried(way, step):
                    hop(way, step, which, origin_of(way, step)).wait_recv()
                    if step < half and which in carried(way, step + 1):
                        copy = hop(way, step + 1, which, origin_of(way, step))
                        copy.start()
                        sent.append(copy)
        for which in (0, 1):
            for way in (0, 1):
                if which in carried(way, step):
                    multiply(which, origin_of(way, step))
    for copy in sent:
        copy.wait_send()

    waits = []
    ones = []
    for a in (0, 1):
        for yy in range(ny):
            send_one[a, yy] = total[a, yy * 2 + 1 - core].astype(BF16)
        copy = pltpu.make_async_remote_copy(
            src_ref=send_one.at[a], dst_ref=recv_one.at[a],
            send_sem=one_send.at[a], recv_sem=one_recv.at[a],
            device_id={"row": sibling}, device_id_type=MESH,
        )
        copy.start()
        ones.append(copy)
    twos = []
    for a in (0, 1):
        ones[a].wait_recv()
        for i, other in enumerate(others):
            yt = other // 2
            send_two[a, i] = (total[a, other] + recv_one[a, yt].astype(F32)).astype(BF16)
            copy = pltpu.make_async_remote_copy(
                src_ref=send_two.at[a, i], dst_ref=recv_two.at[a, i],
                send_sem=two_send.at[a, i], recv_sem=two_recv.at[a, i],
                device_id={"row": other}, device_id_type=MESH,
            )
            copy.start()
            twos.append(copy)
        total[a, me_r] = total[a, me_r] + recv_one[a, y].astype(F32)
    for copy in twos:
        copy.wait_recv()

    @pl.loop(0, rows // 16)
    def _(i):
        part = pl.ds(pl.multiple_of(i * 16, 16), 16)
        pre = total[0, me_r, part, :]
        grad = total[1, me_r, part, :]
        for j in range(ny - 1):
            pre = pre + recv_two[0, j, part, :].astype(F32)
            grad = grad + recv_two[1, j, part, :].astype(F32)
        activated, slope = gelu_pair(pre)
        ac_all[me_r, part, :] = activated.astype(BF16)
        pg_all[me_r, part, :] = (grad * slope).astype(BF16)

    outs = (pg_all, ac_all)

    def spread(a, lane, slot, target):
        return pltpu.make_async_remote_copy(
            src_ref=outs[a].at[slot], dst_ref=outs[a].at[slot],
            send_sem=out_send.at[a, lane], recv_sem=out_recv.at[a, lane],
            device_id={"row": target}, device_id_type=MESH,
        )

    last = []
    for a in (0, 1):
        for i, other in enumerate(others):
            copy = spread(a, i, me_r, other)
            copy.start()
            last.append(copy)
    for a in (0, 1):
        copy = spread(a, ny - 1, me_r, sibling)
        copy.start()
        last.append(copy)
    for a in (0, 1):
        for i in range(ny - 1):
            source = lax.rem(y - (i + 1) + ny, ny)
            spread(a, i, source * 2 + core, others[i]).wait_recv()
            copy = spread(a, ny + i, source * 2 + core, sibling)
            copy.start()
            last.append(copy)
    for a in (0, 1):
        spread(a, ny - 1, sibling, sibling).wait_recv()
        for i in range(ny - 1):
            source = lax.rem(y - (i + 1) + ny, ny)
            spread(a, ny + i, source * 2 + 1 - core, sibling).wait_recv()
    for copy in ones + twos + last:
        copy.wait_send()


def forward(tokens, cotangent, w_expand, w_reduce, nrow, ncol):
    rows, wide = tokens.shape
    k, depth, width = w_expand.shape
    ny = nrow // 2
    half = ncol // 2
    any_spec = pl.BlockSpec(memory_space=pl.ANY)
    vmem = pl.BlockSpec(memory_space=pltpu.VMEM)
    dma = pltpu.SemaphoreType.DMA
    return pl.pallas_call(
        functools.partial(forward_kernel, nrow, ncol),
        out_shape=[jax.ShapeDtypeStruct((ncol, rows, wide), BF16)] * 2
        + [jax.ShapeDtypeStruct((nrow, rows, width), BF16)] * 2,
        in_specs=[vmem, vmem, any_spec, any_spec],
        out_specs=[vmem] * 4,
        scratch_shapes=[
            pltpu.VMEM((2, k, depth, width), BF16),
            pltpu.VMEM((2, nrow, rows, width), F32),
            pltpu.VMEM((2, ny, rows, width), BF16),
            pltpu.VMEM((2, ny, rows, width), BF16),
            pltpu.VMEM((2, ny - 1, rows, width), BF16),
            pltpu.VMEM((2, ny - 1, rows, width), BF16),
            dma((2,)),
            dma((2, half, 2)),
            dma((2, half, 2)),
            dma((2,)),
            dma((2,)),
            dma((2, ny - 1)),
            dma((2, ny - 1)),
            dma((2, 2 * ny - 1)),
            dma((2, 2 * ny - 1)),
        ],
        compiler_params=pltpu.CompilerParams(
            collective_id=0, has_side_effects=True, vmem_limit_bytes=58 * 2**20
        ),
        name="forward",
    )(tokens, cotangent, w_expand, w_reduce)


def back_kernel(nrow, ncol, pg_ref, we_ref, out_ref, send, recv, send_sem, recv_sem):
    half = ncol // 2
    rows = out_ref.shape[0]
    mid = rows // 2
    place = ring_place(lax.axis_index("col"), ncol)
    right, left = ring_col(place + 1, ncol), ring_col(place - 1, ncol)
    greet([{"col": left}, {"col": right}])
    halves = (pl.ds(0, mid), pl.ds(mid, mid))

    def partial_sum(offset):
        slot = ring_col(place + offset, ncol)
        return lax.dot_general(
            pg_ref[slot % nrow], we_ref[slot // nrow],
            (((1,), (1,)), ((), ())), preferred_element_type=F32,
        )

    def hop(way, step):
        src, dst = send.at[way, step], recv.at[way, step]
        if step == 0:
            src, dst = src.at[halves[way]], dst.at[halves[way]]
        return pltpu.make_async_remote_copy(
            src_ref=src, dst_ref=dst,
            send_sem=send_sem.at[way, step], recv_sem=recv_sem.at[way, step],
            device_id={"col": right if way == 0 else left}, device_id_type=MESH,
        )

    first = partial_sum(half)
    copies = []
    for way in (0, 1):
        send[way, 0, halves[way], :] = first[way * mid:(way + 1) * mid].astype(BF16)
        copy = hop(way, 0)
        copy.start()
        copies.append(copy)
    for step in range(1, half):
        for way in (0, 1):
            mine = partial_sum(half - step if way == 0 else step - half)
            hop(way, step - 1).wait_recv()
            if step == 1:
                came = mine[way * mid:(way + 1) * mid] + recv[way, 0, halves[way], :].astype(F32)
                send[way, step, halves[way], :] = came.astype(BF16)
                send[way, step, halves[1 - way], :] = mine[
                    (1 - way) * mid:(2 - way) * mid
                ].astype(BF16)
            else:
                send[way, step] = (mine + recv[way, step - 1].astype(F32)).astype(BF16)
            copy = hop(way, step)
            copy.start()
            copies.append(copy)
    mine = partial_sum(0)
    for way in (0, 1):
        hop(way, half - 1).wait_recv()
        mine = mine + recv[way, half - 1].astype(F32)
    out_ref[...] = mine.astype(BF16)
    for copy in copies:
        copy.wait_send()


def backward(pre_grad, w_expand, nrow, ncol):
    rows = pre_grad.shape[1]
    depth = w_expand.shape[1]
    half = ncol // 2
    vmem = pl.BlockSpec(memory_space=pltpu.VMEM)
    dma = pltpu.SemaphoreType.DMA
    return pl.pallas_call(
        functools.partial(back_kernel, nrow, ncol),
        out_shape=jax.ShapeDtypeStruct((rows, depth), BF16),
        in_specs=[vmem, vmem],
        out_specs=vmem,
        scratch_shapes=[
            pltpu.VMEM((2, half, rows, depth), BF16),
            pltpu.VMEM((2, half, rows, depth), BF16),
            dma((2, half)),
            dma((2, half)),
        ],
        compiler_params=pltpu.CompilerParams(
            collective_id=1, has_side_effects=True, vmem_limit_bytes=48 * 2**20
        ),
        name="backward",
    )(pre_grad, w_expand)


def adam_kernel(
    x_ref, g_ref, w_ref, mq_ref, ms_ref, vq_ref, vs_ref,
    nw_ref, mn_ref, msn_ref, vn_ref, vsn_ref,
    grad, mean, var,
):
    row = pl.program_id(1)
    grad[...] = lax.dot_general(
        x_ref[0], g_ref[...], (((0,), (0,)), ((), ())), preferred_element_type=F32
    )
    size, cols = grad.shape
    here = pl.ds(row, 1)
    mean_scale = beta_one * ms_ref[here, :]
    var_scale = beta_two * vs_ref[here, :]
    chunk = 16

    def first(i, tops):
        top_m, top_v = tops
        part = pl.ds(pl.multiple_of(i * chunk, chunk), chunk)
        g = grad[part, :]
        m = mean_scale * mq_ref[part, :].astype(F32) + (1.0 - beta_one) * g
        v = var_scale * vq_ref[part, :].astype(F32) + (1.0 - beta_two) * g * g
        mean[part, :] = m
        var[part, :] = v
        mean_hat = m * (1.0 / (1.0 - beta_one**STEP))
        var_hat = v * (1.0 / (1.0 - beta_two**STEP))
        old = w_ref[part, :].astype(F32)
        step = mean_hat / (jnp.sqrt(var_hat) + adam_eps) + decay_rate * old
        nw_ref[part, :] = (old - learn_rate * step).astype(BF16)
        return jnp.maximum(top_m, jnp.abs(m)), jnp.maximum(top_v, jnp.abs(v))

    zero = jnp.zeros((chunk, cols), F32)
    top_m, top_v = lax.fori_loop(0, size // chunk, first, (zero, zero))
    top_m = jnp.max(top_m, axis=0, keepdims=True) + scale_eps
    top_v = jnp.max(top_v, axis=0, keepdims=True) + scale_eps
    msn_ref[here, :] = top_m
    vsn_ref[here, :] = top_v
    inv_m, inv_v = 1.0 / top_m, 1.0 / top_v

    def second(i, carry):
        part = pl.ds(pl.multiple_of(i * chunk, chunk), chunk)
        mn_ref[part, :] = (mean[part, :] * inv_m).astype(BF16)
        vn_ref[part, :] = (var[part, :] * inv_v).astype(BF16)
        return carry

    lax.fori_loop(0, size // chunk, second, 0)


def adam_step(x, grads, weight, mean_q, mean_scale, var_q, var_scale):
    rows, width = weight.shape
    blocks = mean_scale.shape[0]
    size = rows // blocks
    count = x.shape[1]
    per = x.shape[2] // size
    cols = 512 if width % 512 == 0 else 128
    tile = pl.BlockSpec((size, cols), lambda j, i: (i, j))
    scale = pl.BlockSpec((blocks, cols), lambda j, i: (0, j))
    big = jax.ShapeDtypeStruct((rows, width), BF16)
    small = jax.ShapeDtypeStruct((blocks, width), F32)
    return pl.pallas_call(
        adam_kernel,
        grid=(width // cols, blocks),
        in_specs=[
            pl.BlockSpec((1, count, size), lambda j, i: (i // per, 0, i % per)),
            pl.BlockSpec((count, cols), lambda j, i: (0, j)),
            tile, tile, scale, tile, scale,
        ],
        out_specs=[tile, tile, scale, tile, scale],
        out_shape=[big, big, small, big, small],
        scratch_shapes=[pltpu.VMEM((size, cols), F32)] * 3,
        compiler_params=pltpu.CompilerParams(vmem_limit_bytes=40 * 2**20),
        cost_estimate=pl.CostEstimate(
            flops=2 * count * rows * width, bytes_accessed=14 * rows * width, transcendentals=0
        ),
        name="adam",
    )(x, grads, weight, mean_q, mean_scale, var_q, var_scale)


def local(
    nrow, ncol,
    tokens, cotangent,
    w_expand, w_reduce,
    expand_mean, expand_mean_scale, expand_var, expand_var_scale,
    reduce_mean, reduce_mean_scale, reduce_var, reduce_var_scale,
):
    k = ncol // nrow
    rows, depth = tokens.shape
    width = w_expand.shape[1]
    size = w_expand.shape[0] // expand_mean_scale.shape[0]
    moves = []
    for r in range(nrow):
        for c in range(ncol):
            moves.append((r * ncol + c, (c // k) * ncol + (c % k) * nrow + r))
    returns = [(b, a) for a, b in moves]
    moved_tokens = lax.ppermute(tokens, ("row", "col"), moves)
    moved_cot = lax.ppermute(cotangent, ("row", "col"), moves)
    expand_parts = w_expand.reshape(k, depth, width)
    tok_all, cot_all, pre_grad, activated = forward(
        moved_tokens, moved_cot, expand_parts, w_reduce.reshape(k, depth, width), nrow, ncol
    )
    summed = backward(pre_grad, expand_parts, nrow, ncol)
    grad_tokens = lax.ppermute(summed, ("row", "col"), returns)

    def whole(x):
        x = x.reshape(k, nrow * rows, depth)
        if depth % size:
            x = x.transpose(1, 0, 2).reshape(1, nrow * rows, k * depth)
        return x

    first = adam_step(
        whole(tok_all), pre_grad.reshape(nrow * rows, width), w_expand,
        expand_mean, expand_mean_scale, expand_var, expand_var_scale,
    )
    second = adam_step(
        whole(cot_all), activated.reshape(nrow * rows, width), w_reduce,
        reduce_mean, reduce_mean_scale, reduce_var, reduce_var_scale,
    )
    return (grad_tokens, *first, *second)


def solution(mesh):
    nrow, ncol = mesh.shape["row"], mesh.shape["col"]
    return jax.shard_map(
        functools.partial(local, nrow, ncol),
        mesh=mesh,
        in_specs=(P("row", "col"),) * 12,
        out_specs=(P("row", "col"),) * 11,
        check_vma=False,
    )
```

```python
import functools

import jax
import jax.numpy as jnp
from jax import lax
from jax.experimental import pallas as pl
from jax.experimental.pallas import tpu as pltpu
from jax.sharding import PartitionSpec as P

STEP = 10


beta_one = 0.9
beta_two = 0.999
adam_eps = 1e-08
learn_rate = 0.001
decay_rate = 0.1
scale_eps = 1e-06

MESH = pl.DeviceIdType.MESH
F32 = jnp.float32
BF16 = jnp.bfloat16


def gelu_pair(pre_act):
    cdf_part = 0.5 * (1.0 + lax.erf(pre_act * 0.7071067811865476))
    slope = cdf_part + pre_act * jnp.exp(-0.5 * pre_act * pre_act) * 0.3989422804014327
    return (pre_act * cdf_part, slope)


def ring_place(col, n):
    half, odd = col // 2, col % 2
    return half * (1 - odd) + (n - 1 - half) * odd


def ring_col(place, n):
    place = lax.rem(place + 2 * n, n)
    back = place // (n // 2)
    return (1 - back) * 2 * place + back * (2 * (n - 1 - place) + 1)


def greet(peers):
    barrier = pltpu.get_barrier_semaphore()
    for peer in peers:
        pl.semaphore_signal(barrier, inc=1, device_id=peer, device_id_type=MESH)
    pl.semaphore_wait(barrier, len(peers))


def forward_kernel(
    nrow, ncol,
    tok_ref, cot_ref, we_ref, wr_ref,
    tok_all, cot_all, pg_all, ac_all,
    w_tile, total, recv_one, send_two, recv_two, slope_ref,
    w_sem, ring_send, ring_recv, one_send, one_recv, two_send, two_recv, out_send, out_recv,
):
    ny = nrow // 2
    half = ncol // 2
    rows = tok_ref.shape[0]
    mid = rows // 2
    width = w_tile.shape[3]
    me_c = lax.axis_index("col")
    me_r = lax.axis_index("row")
    y, core = me_r // 2, me_r % 2
    place = ring_place(me_c, ncol)
    right, left = ring_col(place + 1, ncol), ring_col(place - 1, ncol)
    sibling = y * 2 + 1 - core
    others = [lax.rem(y + step, ny) * 2 + core for step in range(1, ny)]
    sources = [lax.rem(y - step + ny, ny) for step in range(1, ny)]

    loads = [
        pltpu.make_async_copy(ref, w_tile.at[i], w_sem.at[i])
        for i, ref in enumerate((we_ref, wr_ref))
    ]
    for load in loads:
        load.start()
    greet([{"col": left}, {"col": right}, {"row": sibling}] + [{"row": o} for o in others])

    gathered = (tok_all, cot_all)
    tok_all[me_c] = tok_ref[...]
    cot_all[me_c] = cot_ref[...]
    sent = []

    def hop(which, way, step, origin):
        block = gathered[which].at[ring_col(place + origin, ncol)]
        if step == half:
            block = block.at[pl.ds(way * mid, mid)]
        return pltpu.make_async_remote_copy(
            src_ref=block,
            dst_ref=block,
            send_sem=ring_send.at[which, way, step - 1],
            recv_sem=ring_recv.at[which, way, step - 1],
            device_id={"col": right if way == 0 else left},
            device_id_type=MESH,
        )

    def launch(copy):
        copy.start()
        sent.append(copy)

    def multiply(which, origin):
        slot = ring_col(place + origin, ncol)
        part, band = slot // nrow, slot % nrow
        tile = width // 3

        @pl.loop(0, 3)
        def _(j):
            cols = pl.ds(pl.multiple_of(j * tile, 128), tile)
            total[which, band, :, cols] += jnp.dot(
                gathered[which][slot], w_tile[which, part, :, cols], preferred_element_type=F32
            )

    def ring_step(which, step, between=None):
        for way in (0, 1):
            origin = -step if way == 0 else step
            hop(which, way, step, origin).wait_recv()
            if step < half:
                launch(hop(which, way, step + 1, origin))
        if between is not None:
            between()
        multiply(which, -step)
        if step < half:
            multiply(which, step)

    def core_swap(a, yy):
        return pltpu.make_async_remote_copy(
            src_ref=total.at[a, yy * 2 + 1 - core], dst_ref=recv_one.at[a, yy],
            send_sem=one_send.at[a, yy], recv_sem=one_recv.at[a, yy],
            device_id={"row": sibling}, device_id_type=MESH,
        )

    def y_swap(a, i):
        return pltpu.make_async_remote_copy(
            src_ref=send_two.at[a, i], dst_ref=recv_two.at[a, i],
            send_sem=two_send.at[a, i], recv_sem=two_recv.at[a, i],
            device_id={"row": others[i]}, device_id_type=MESH,
        )

    def start_cores(a):
        for yy in range(ny):
            launch(core_swap(a, yy))

    def start_y(a):
        for yy in range(ny):
            core_swap(a, yy).wait_recv()
        for i, other in enumerate(others):

            @pl.loop(0, rows // 16)
            def _(n):
                part = pl.ds(pl.multiple_of(n * 16, 16), 16)
                send_two[a, i, part, :] = (
                    total[a, other, part, :] + recv_one[a, other // 2, part, :]
                ).astype(BF16)

            launch(y_swap(a, i))

    def summed(a, part):
        value = total[a, me_r, part, :] + recv_one[a, y, part, :]
        for i in range(ny - 1):
            value = value + recv_two[a, i, part, :].astype(F32)
        return value

    outs = (pg_all, ac_all)

    def spread(a, lane, slot, target):
        return pltpu.make_async_remote_copy(
            src_ref=outs[a].at[slot], dst_ref=outs[a].at[slot],
            send_sem=out_send.at[a, lane], recv_sem=out_recv.at[a, lane],
            device_id={"row": target}, device_id_type=MESH,
        )

    def start_spread(a):
        for i, other in enumerate(others):
            launch(spread(a, i, me_r, other))
        launch(spread(a, ny - 1, me_r, sibling))

    def pass_on(a):
        for i in range(ny - 1):
            slot = sources[i] * 2 + core
            spread(a, i, slot, others[i]).wait_recv()
            launch(spread(a, ny + i, slot, sibling))

    def end_spread(a):
        spread(a, ny - 1, sibling, sibling).wait_recv()
        for i in range(ny - 1):
            spread(a, ny + i, sources[i] * 2 + 1 - core, sibling).wait_recv()

    def activate():
        for i in range(ny - 1):
            y_swap(0, i).wait_recv()

        @pl.loop(0, rows // 16)
        def _(n):
            part = pl.ds(pl.multiple_of(n * 16, 16), 16)
            activated, slope = gelu_pair(summed(0, part))
            ac_all[me_r, part, :] = activated.astype(BF16)
            slope_ref[part, :] = slope

        start_spread(1)

    for way in (0, 1):
        launch(hop(0, way, 1, 0))
    total[...] = jnp.zeros_like(total)
    for load in loads:
        load.wait()
    multiply(0, 0)
    for step in range(1, half + 1):
        if step == half:
            for way in (0, 1):
                launch(hop(1, way, 1, 0))
        ring_step(0, step)
    start_cores(0)
    multiply(1, 0)
    for step in range(1, half + 1):
        if step == half:
            ring_step(1, step, activate)
        elif step == 1:
            ring_step(1, step, lambda: start_y(0))
        else:
            ring_step(1, step)
    start_cores(1)
    start_y(1)
    pass_on(1)
    for i in range(ny - 1):
        y_swap(1, i).wait_recv()

    @pl.loop(0, rows // 16)
    def _(n):
        part = pl.ds(pl.multiple_of(n * 16, 16), 16)
        pg_all[me_r, part, :] = (summed(1, part) * slope_ref[part, :]).astype(BF16)

    start_spread(0)
    pass_on(0)
    end_spread(1)
    end_spread(0)
    for copy in sent:
        copy.wait_send()


def forward(tokens, cotangent, w_expand, w_reduce, nrow, ncol):
    rows, wide = tokens.shape
    k, depth, width = w_expand.shape
    ny = nrow // 2
    half = ncol // 2
    any_spec = pl.BlockSpec(memory_space=pl.ANY)
    vmem = pl.BlockSpec(memory_space=pltpu.VMEM)
    dma = pltpu.SemaphoreType.DMA
    return pl.pallas_call(
        functools.partial(forward_kernel, nrow, ncol),
        out_shape=[jax.ShapeDtypeStruct((ncol, rows, wide), BF16)] * 2
        + [jax.ShapeDtypeStruct((nrow, rows, width), BF16)] * 2,
        in_specs=[vmem, vmem, any_spec, any_spec],
        out_specs=[vmem] * 4,
        scratch_shapes=[
            pltpu.VMEM((2, k, depth, width), BF16),
            pltpu.VMEM((2, nrow, rows, width), F32),
            pltpu.VMEM((2, ny, rows, width), F32),
            pltpu.VMEM((2, ny - 1, rows, width), BF16),
            pltpu.VMEM((2, ny - 1, rows, width), BF16),
            pltpu.VMEM((rows, width), F32),
            dma((2,)),
            dma((2, 2, half)),
            dma((2, 2, half)),
            dma((2, ny)),
            dma((2, ny)),
            dma((2, ny - 1)),
            dma((2, ny - 1)),
            dma((2, 2 * ny - 1)),
            dma((2, 2 * ny - 1)),
        ],
        compiler_params=pltpu.CompilerParams(
            collective_id=0, has_side_effects=True, vmem_limit_bytes=58 * 2**20
        ),
        name="forward",
    )(tokens, cotangent, w_expand, w_reduce)


def backward(pre_grad, w_expand, ncol, beside):
    nrow, rows, _ = pre_grad.shape
    half = ncol // 2
    mid = rows // 2
    place = ring_place(lax.axis_index("col"), ncol)
    cycle = [2 * p if p < half else 2 * (ncol - 1 - p) + 1 for p in range(ncol)]
    rightward = [(cycle[p], cycle[(p + 1) % ncol]) for p in range(ncol)]
    leftward = [(b, a) for a, b in rightward]

    def partial_sum(offset):
        slot = ring_col(place + offset, ncol)
        band = lax.dynamic_index_in_dim(pre_grad, slot % nrow, 0, keepdims=False)
        part = lax.dynamic_index_in_dim(w_expand, slot // nrow, 0, keepdims=False)
        return lax.dot_general(band, part, (((1,), (1,)), ((), ())), preferred_element_type=F32)

    first = partial_sum(half).astype(BF16)
    going = [first[:mid], first[mid:]]
    for step in range(1, half + 1):
        came = [lax.ppermute(going[0], "col", rightward), lax.ppermute(going[1], "col", leftward)]
        came = [x.astype(F32) for x in came]
        if step == 1:
            came = [jnp.pad(came[0], ((0, mid), (0, 0))), jnp.pad(came[1], ((mid, 0), (0, 0)))]
        if step < half:
            mine = beside((partial_sum(half - step), partial_sum(step - half)))
            going = [(m + c).astype(BF16) for m, c in zip(mine, came)]
    (mine,) = beside((partial_sum(0),))
    return (mine + came[0] + came[1]).astype(BF16)


def adam_kernel(
    x_ref, g_ref, w_ref, mq_ref, ms_ref, vq_ref, vs_ref,
    nw_ref, mn_ref, msn_ref, vn_ref, vsn_ref,
    grad, mean, var,
):
    row = pl.program_id(1)
    grad[...] = lax.dot_general(
        x_ref[0], g_ref[...], (((0,), (0,)), ((), ())), preferred_element_type=F32
    )
    size, cols = grad.shape
    here = pl.ds(row, 1)
    mean_scale = beta_one * ms_ref[here, :]
    var_scale = beta_two * vs_ref[here, :]
    chunk = 16

    def first(i, tops):
        top_m, top_v = tops
        part = pl.ds(pl.multiple_of(i * chunk, chunk), chunk)
        g = grad[part, :]
        m = mean_scale * mq_ref[part, :].astype(F32) + (1.0 - beta_one) * g
        v = var_scale * vq_ref[part, :].astype(F32) + (1.0 - beta_two) * g * g
        mean[part, :] = m
        var[part, :] = v
        mean_hat = m * (1.0 / (1.0 - beta_one**STEP))
        var_hat = v * (1.0 / (1.0 - beta_two**STEP))
        old = w_ref[part, :].astype(F32)
        step = mean_hat / (jnp.sqrt(var_hat) + adam_eps) + decay_rate * old
        nw_ref[part, :] = (old - learn_rate * step).astype(BF16)
        return jnp.maximum(top_m, jnp.abs(m)), jnp.maximum(top_v, jnp.abs(v))

    zero = jnp.zeros((chunk, cols), F32)
    top_m, top_v = lax.fori_loop(0, size // chunk, first, (zero, zero))
    top_m = jnp.max(top_m, axis=0, keepdims=True) + scale_eps
    top_v = jnp.max(top_v, axis=0, keepdims=True) + scale_eps
    msn_ref[here, :] = top_m
    vsn_ref[here, :] = top_v
    inv_m, inv_v = 1.0 / top_m, 1.0 / top_v

    def second(i, carry):
        part = pl.ds(pl.multiple_of(i * chunk, chunk), chunk)
        mn_ref[part, :] = (mean[part, :] * inv_m).astype(BF16)
        vn_ref[part, :] = (var[part, :] * inv_v).astype(BF16)
        return carry

    lax.fori_loop(0, size // chunk, second, 0)


def adam_piece(state, begin, number, outs, carried):
    x, grads, weight, mean_q, mean_scale = state[:5]
    rows, width = weight.shape
    blocks = mean_scale.shape[0]
    size = rows // blocks
    count = x.shape[1]
    per = x.shape[2] // size
    cols = adam_cols(width)
    big = jax.ShapeDtypeStruct((rows, width), BF16)
    small = jax.ShapeDtypeStruct((blocks, width), F32)
    tile = pl.BlockSpec((size, cols), lambda j, i: (i, j + begin))
    scale = pl.BlockSpec((blocks, cols), lambda j, i: (0, j + begin))
    held = (*outs, *carried)
    anywhere = pl.BlockSpec(memory_space=pl.ANY)
    first_out = 0 if outs else 5

    def body(*refs):
        start = 7 + len(held)
        adam_kernel(*refs[:7], *refs[start:start + 5], *refs[-3:])

    result = pl.pallas_call(
        body,
        grid=(number, blocks),
        in_specs=[
            pl.BlockSpec((1, count, size), lambda j, i: (i // per, 0, i % per)),
            pl.BlockSpec((count, cols), lambda j, i: (0, j + begin)),
            tile, tile, scale, tile, scale,
        ] + [anywhere] * len(held),
        out_specs=[tile, tile, scale, tile, scale] + [anywhere] * len(carried),
        out_shape=[big, big, small, big, small]
        + [jax.ShapeDtypeStruct(c.shape, c.dtype) for c in carried],
        scratch_shapes=[pltpu.VMEM((size, cols), F32)] * 3,
        input_output_aliases={7 + i: first_out + i for i in range(len(held))},
        compiler_params=pltpu.CompilerParams(vmem_limit_bytes=40 * 2**20),
        cost_estimate=pl.CostEstimate(
            flops=2 * count * rows * cols * number,
            bytes_accessed=14 * rows * cols * number,
            transcendentals=0,
        ),
        name="adam",
    )(*state, *held)
    return tuple(result[:5]), tuple(result[5:])


def adam_cols(width):
    return 512 if width % 512 == 0 else 128


def local(
    nrow, ncol,
    tokens, cotangent,
    w_expand, w_reduce,
    expand_mean, expand_mean_scale, expand_var, expand_var_scale,
    reduce_mean, reduce_mean_scale, reduce_var, reduce_var_scale,
):
    k = ncol // nrow
    rows, depth = tokens.shape
    width = w_expand.shape[1]
    size = w_expand.shape[0] // expand_mean_scale.shape[0]
    moves = []
    for r in range(nrow):
        for c in range(ncol):
            moves.append((r * ncol + c, (c // k) * ncol + (c % k) * nrow + r))
    returns = [(b, a) for a, b in moves]
    moved_tokens = lax.ppermute(tokens, ("row", "col"), moves)
    moved_cot = lax.ppermute(cotangent, ("row", "col"), moves)
    expand_parts = w_expand.reshape(k, depth, width)
    tok_all, cot_all, pre_grad, activated = forward(
        moved_tokens, moved_cot, expand_parts, w_reduce.reshape(k, depth, width), nrow, ncol
    )
    def whole(x):
        x = x.reshape(k, nrow * rows, depth)
        if depth % size:
            x = x.transpose(1, 0, 2).reshape(1, nrow * rows, k * depth)
        return x

    states = (
        (
            whole(cot_all), activated.reshape(nrow * rows, width), w_reduce,
            reduce_mean, reduce_mean_scale, reduce_var, reduce_var_scale,
        ),
        (
            whole(tok_all), pre_grad.reshape(nrow * rows, width), w_expand,
            expand_mean, expand_mean_scale, expand_var, expand_var_scale,
        ),
    )
    tiles = width // adam_cols(width)
    done = [(), ()]
    pieces = [(0, j, 1) for j in range(tiles)] + [(1, 0, 1), (1, 1, tiles - 1)]

    def run_piece(carried):
        which, begin, number = pieces.pop(0)
        done[which], carried = adam_piece(states[which], begin, number, done[which], carried)
        return carried

    def beside(carried):
        return run_piece(carried) if len(pieces) > 1 else carried

    summed = backward(pre_grad, expand_parts, ncol, beside)
    grad_tokens = lax.ppermute(summed, ("row", "col"), returns)
    while pieces:
        run_piece(())
    second, first = done
    return (grad_tokens, *first, *second)


def solution(mesh):
    nrow, ncol = mesh.shape["row"], mesh.shape["col"]
    return jax.shard_map(
        functools.partial(local, nrow, ncol),
        mesh=mesh,
        in_specs=(P("row", "col"),) * 12,
        out_specs=(P("row", "col"),) * 11,
        check_vma=False,
    )
```
